128 devices in a mesh: tm: 4 (over y), lat: 4 (over x_lo, core), lon: 8 (over z, x_hi).
Axes of the slice: x: 4 (x_hi: 2, x_lo: 2; x = x_hi * 2 + x_lo), y: 4, z: 4, core: 2. Of those that a mesh axis runs over, the one named last changes fastest.
Arguments:
- latents: bfloat16 [4, 64, 128, 1536], P('tm', 'lat', 'lon'), may hold values from -450 to 450
- ada_shift: float32 [1536], replicated, may hold values from -3 to 3
- ada_scale: float32 [1536], replicated, may hold values from -0.5 to 0.5
- ada_gate: float32 [1536], replicated, may hold values from 0.5 to 1.5
- w_query: bfloat16 [1536, 1536], replicated, may hold values from -2 to 2
- w_key: bfloat16 [1536, 1536], replicated, may hold values from -2 to 2
- w_value: bfloat16 [1536, 1536], replicated, may hold values from -0.15625 to 0.15625
- w_out: bfloat16 [1536, 1536], replicated, may hold values from -0.15625 to 0.15625
- query_gain: float32 [1536], replicated, may hold values from 0.3 to 6.5
- key_gain: float32 [1536], replicated, may hold values from 0.3 to 6.5
Outputs:
- branch_out: bfloat16 [4, 64, 128, 1536], P('tm', 'lat', 'lon')
The draws below stay inside these ranges and needn't reach their ends.
All inputs are finite; a program needn't handle non-finite values.
Results may differ from the reference program's by a relative error of at most 0.0075.
Values may be sent and summed in bfloat16 or wider, within the bound.
A program may use at most 128 MiB of HBM per device.

```python
import jax
import jax.numpy as jnp
from jax import lax

HEADS = 12
HEAD_DIM = 128
D = 1536
NT = 4
NLAT = 64
NLON = 128


def shared_parts(key):
    spread_key = jax.random.fold_in(key, 17)
    spread = jnp.exp(jax.random.uniform(spread_key, (1, D), jnp.float32, 0.0, jnp.log(10.0)))
    return spread


def head_gains(key, head_low, head_high, dim_low, dim_high):
    head_key, dim_key = jax.random.split(key)
    per_head = jnp.exp(jax.random.uniform(head_key, (HEADS, 1), jnp.float32, jnp.log(head_low), jnp.log(head_high)))
    per_dim = jax.random.uniform(dim_key, (HEADS, HEAD_DIM), jnp.float32, dim_low, dim_high)
    return (per_head * per_dim).reshape(D)


def draw_latents(key, part):
    key = jax.random.fold_in(key, 1)
    col_key, row_key, base_key = jax.random.split(key, 3)
    columns = jnp.exp(jax.random.uniform(col_key, (1, 1, 1, D), jnp.float32, 0.0, jnp.log(10.0)))
    row_scales = jnp.exp(jax.random.uniform(row_key, (NT, NLAT, NLON, 1), jnp.float32, 0.0, jnp.log(10.0)))
    values = jnp.clip(jax.random.normal(base_key, (NT, NLAT, NLON, D), jnp.float32), -4.0, 4.0)
    return (values * columns * row_scales).astype(jnp.bfloat16)


def draw_w_query(key, part):
    spread = shared_parts(key)
    key = jax.random.fold_in(key, 2)
    own = jnp.clip(jax.random.normal(key, (D, D), jnp.float32), -5.0, 5.0)
    mixed = own
    return (mixed * spread * D ** (-0.5) / 4.0).astype(jnp.bfloat16)


def draw_w_key(key, part):
    spread = shared_parts(key)
    key = jax.random.fold_in(key, 3)
    own = jnp.clip(jax.random.normal(key, (D, D), jnp.float32), -5.0, 5.0)
    mixed = own
    return (mixed * spread * D ** (-0.5) / 4.0).astype(jnp.bfloat16)


def draw_query_gain(key, part):
    key = jax.random.fold_in(key, 4)
    return head_gains(key, 0.5, 2.0, 0.7, 1.3)


def draw_key_gain(key, part):
    key = jax.random.fold_in(key, 5)
    return head_gains(key, 0.5, 2.0, 0.7, 1.3)


def gaussian(own_key, dims, width, most, kind=jnp.bfloat16):
    array = width * jax.random.normal(own_key, dims, jnp.float32)
    return jnp.clip(array, min=-most, max=most).astype(kind)


def setup_inputs(seed: int = 0) -> dict:
    streams_of = jax.random.split(jax.random.key(seed), 11)
    return {
        "latents": draw_latents(jax.random.fold_in(streams_of[10], 71), 0),
        "ada_shift": gaussian(streams_of[1], (D,), 0.5, 3.0, jnp.float32),
        "ada_scale": jnp.clip(jax.random.uniform(streams_of[2], (D,), jnp.float32, -0.5, 0.5), -0.5, 0.5),
        "ada_gate": jnp.clip(jax.random.uniform(streams_of[3], (D,), jnp.float32, 0.5, 1.5), 0.5, 1.5),
        "w_query": draw_w_query(jax.random.fold_in(streams_of[10], 71), 0),
        "w_key": draw_w_key(jax.random.fold_in(streams_of[10], 71), 0),
        "w_value": gaussian(streams_of[6], (D, D), D ** -0.5, 0.15625),
        "w_out": gaussian(streams_of[7], (D, D), D ** -0.5, 0.15625),
        "query_gain": draw_query_gain(jax.random.fold_in(streams_of[10], 71), 0),
        "key_gain": draw_key_gain(jax.random.fold_in(streams_of[10], 71), 0),
    }


def modulate(latents, ada_shift, ada_scale):
    values_f = latents.astype(jnp.float32)
    mean_value = lax.optimization_barrier(jnp.mean(values_f, axis=-1, keepdims=True))
    centred = values_f - mean_value
    variance = lax.optimization_barrier(jnp.mean(centred * centred, axis=-1, keepdims=True))
    return (centred * lax.rsqrt(variance + 1e-06) * (1.0 + ada_scale) + ada_shift).astype(jnp.bfloat16)

def rms_gain(projected, gain_vector):
    mean_square = lax.optimization_barrier(jnp.mean(projected * projected, axis=-1, keepdims=True))
    return (projected * lax.rsqrt(mean_square + 1e-06) * gain_vector).astype(jnp.bfloat16)

def reference(latents, ada_shift, ada_scale, ada_gate, w_query, w_key, w_value, w_out, query_gain, key_gain):
    frame_count, lat_count, lon_count, model_width = latents.shape
    normed = modulate(latents, ada_shift, ada_scale).reshape(-1, model_width)
    query_rows = rms_gain(jnp.dot(normed, w_query, preferred_element_type=jnp.float32), query_gain)
    key_rows = rms_gain(jnp.dot(normed, w_key, preferred_element_type=jnp.float32), key_gain)
    value_rows = jnp.dot(normed, w_value, preferred_element_type=jnp.float32).astype(jnp.bfloat16)
    head_shape = (frame_count, lat_count, lon_count, HEADS, HEAD_DIM)
    query_full = query_rows.reshape(head_shape).astype(jnp.float32)

    def padded_grid(block):
        block = jnp.pad(block.reshape(head_shape), ((1, 1), (3, 3), (0, 0), (0, 0), (0, 0)))
        return jnp.concatenate([block[:, :, lon_count - 3:], block, block[:, :, :3]], axis=2)
    key_padded = padded_grid(key_rows)
    value_padded = padded_grid(value_rows)
    offsets = jnp.arange(147, dtype=jnp.int32)
    time_pos = jnp.arange(frame_count, dtype=jnp.int32).reshape(-1, 1, 1)
    lat_pos = jnp.arange(lat_count, dtype=jnp.int32).reshape(1, -1, 1)

    def window(padded, offset):
        time_step = offset // 49
        lat_step = offset // 7 % 7
        lon_step = offset % 7
        anchor = jnp.zeros((), jnp.int32)
        shifted = lax.dynamic_slice(padded, (time_step, lat_step, lon_step, anchor, anchor), head_shape)
        in_grid = (time_pos + time_step - 1 >= 0) & (time_pos + time_step - 1 < frame_count) & (lat_pos + lat_step - 3 >= 0) & (lat_pos + lat_step - 3 < lat_count)
        return (shifted, in_grid)

    def score_step(carry, offset):
        shifted, in_grid = window(key_padded, offset)
        dots = lax.optimization_barrier(jnp.sum(query_full * shifted.astype(jnp.float32), axis=-1)) * HEAD_DIM ** (-0.5)
        return (carry, jnp.where(in_grid[..., None], dots, -1e+30))
    all_scores = lax.scan(score_step, None, offsets)[1]
    row_max = lax.optimization_barrier(jnp.max(all_scores, axis=0))
    raw_weights = jnp.exp(all_scores - row_max)
    probs = (raw_weights / lax.optimization_barrier(jnp.sum(raw_weights, axis=0))).astype(jnp.bfloat16)

    def value_step(running, inputs):
        offset, weight = inputs
        shifted, in_grid = window(value_padded, offset)
        return (running + weight.astype(jnp.float32)[..., None] * shifted.astype(jnp.float32), None)
    attended = lax.scan(value_step, jnp.zeros(head_shape, jnp.float32), (offsets, probs))[0]
    attended = attended.astype(jnp.bfloat16).reshape(-1, model_width)
    projected = jnp.dot(attended, w_out, preferred_element_type=jnp.float32) * ada_gate
    return projected.astype(jnp.bfloat16).reshape(latents.shape)
```

```python
import functools
import math

import jax
import jax.numpy as jnp
import numpy as np
from jax import lax
from jax.experimental import pallas as pl
from jax.experimental.pallas import tpu as pltpu
from jax.sharding import PartitionSpec as P

HEADS = 12
HEAD_DIM = 128
D = 1536
SIDE = 16
TOKENS = SIDE * SIDE
KEYS = 1536
BF = jnp.bfloat16
F32 = jnp.float32
MESH = pl.DeviceIdType.MESH
MASKED = -1e30
SCALE = HEAD_DIM ** (-0.5) * math.log2(math.e)

OWN = 0
OWN_HALO = 256
C1 = (512, 608)
C2 = (704, 768)
C3 = (832, 928)
HALOS = (1024, 1280)
HALO_AT = (OWN_HALO, HALOS[0], HALOS[1])
CHUNKS = ((0, 96), (96, 64), (160, 96))
PIECES = ((0, 48), (48, 48), (96, 48), (144, 48), (192, 16), (208, 16), (224, 16), (240, 16))


def center_order():
    order = [(r, c) for c in (0, 1, 2, 13, 14, 15) for r in range(16)]
    order += [(r, c) for r in (0, 1, 2) for c in range(3, 13)]
    order += [(r, c) for r in (13, 14, 15) for c in range(3, 13)]
    order += [(r, c) for r in range(3, 13) for c in range(3, 13)]
    return order


def edge_lists():
    lo, hi, full = (0, 1, 2), (13, 14, 15), range(16)
    north = [(r, c) for r in lo for c in full]
    south = [(r, c) for r in hi for c in full]
    corners = []
    for rows in (lo, hi):
        for cols in (lo, hi):
            corners.append([(r, c) for r in rows for c in cols] + [None] * 7)
    return north, south, corners


def tables():
    order = center_order()
    where = {p: i for i, p in enumerate(order)}
    perm = np.zeros((TOKENS, TOKENS), np.float32)
    for i, (r, c) in enumerate(order):
        perm[i, r * SIDE + c] = 1
    north, south, corners = edge_lists()
    pack_list = north + south + sum(corners, [])
    pack = np.zeros((160, 160), np.float32)
    for i, p in enumerate(pack_list):
        if p is not None:
            pack[i, where[p]] = 1

    def moved(cells, dr, dc):
        return [None if p is None else (p[0] + dr, p[1] + dc) for p in cells]

    lo = [(r, c) for c in (0, 1, 2) for r in range(16)]
    hi = [(r, c) for c in (13, 14, 15) for r in range(16)]
    nw, ne, sw, se = corners
    halo = moved(hi, 0, -16) + moved(lo, 0, 16) + moved(south, -16, 0) + moved(north, 16, 0)
    halo += moved(se, -16, -16) + moved(sw, -16, 16) + moved(ne, 16, -16) + moved(nw, 16, 16)
    keys = order + halo
    for a, n in CHUNKS:
        keys += order[a : a + n] * 2
    keys += halo * 2
    bias = np.full((TOKENS, KEYS), MASKED, np.float32)
    for j, p in enumerate(keys):
        if p is None:
            continue
        for i, (r, c) in enumerate(order):
            if abs(r - p[0]) <= 3 and abs(c - p[1]) <= 3:
                bias[i, j] = 0
    return perm, perm.T.copy(), pack, bias


def kernel(
    x_ref, shift_ref, scale_ref, gate_ref, qgain_ref, kgain_ref, wq_any, wk_any, wv_any, wo_any,
    perm_ref, back_ref, pack_ref, bias_ref, out_ref,
    wq, wk, wv, wo, xs, ks, vs, qs, packed, flat, bias, acc, m_ref, l_ref,
    w_sem, y_send, y_recv, h_send, h_recv,
):
    t, a, o = lax.axis_index("tm"), lax.axis_index("lat"), lax.axis_index("lon")
    west, east = lax.rem(o + 7, 8), lax.rem(o + 1, 8)
    has_prev, has_next = t > 0, t < 3
    has_north, has_south = a > 0, a < 3
    dirs = (
        (None, (t, a, west)), (None, (t, a, east)),
        (has_north, (t, a - 1, o)), (has_south, (t, a + 1, o)),
        (has_north, (t, a - 1, west)), (has_north, (t, a - 1, east)),
        (has_south, (t, a + 1, west)), (has_south, (t, a + 1, east)),
    )
    opposite = (1, 0, 3, 2, 7, 6, 5, 4)
    frames = ((has_prev, (t - 1, a, o)), (has_next, (t + 1, a, o)))

    def when(cond, fn):
        if cond is None:
            fn()
        else:
            pl.when(cond)(fn)

    loads = []
    for i, (src, dst) in enumerate(((wq_any, wq), (wk_any, wk), (wv_any, wv), (wo_any, wo))):
        loads.append(pltpu.make_async_copy(src, dst, w_sem.at[i]))
        loads[-1].start()

    barrier = pltpu.get_barrier_semaphore()
    for cond, dev in dirs + frames:
        when(cond, lambda dev=dev: pl.semaphore_signal(barrier, inc=1, device_id=dev, device_id_type=MESH))

    one = lambda c: jnp.where(c, 1, 0)

    @pl.loop(0, 4)
    def _(i):
        rows = pl.ds(pl.multiple_of(i * 64, 64), 64)
        v = x_ref[rows, :].astype(F32)
        centred = v - jnp.mean(v, axis=-1, keepdims=True)
        var = jnp.mean(centred * centred, axis=-1, keepdims=True)
        flat[rows, :] = (centred * lax.rsqrt(var + 1e-06) * (1.0 + scale_ref[...]) + shift_ref[...]).astype(BF)

    xs[0:TOKENS, :] = jnp.dot(perm_ref[...], flat[...], preferred_element_type=F32).astype(BF)
    pl.semaphore_wait(barrier, 2 + one(has_prev) + one(has_next) + 3 * one(has_north) + 3 * one(has_south))

    def y_copy(chunk, side):
        start, n = CHUNKS[chunk]
        dst = (C1, C2, C3)[chunk][1 - side]
        return pltpu.make_async_remote_copy(
            src_ref=xs.at[start : start + n], dst_ref=xs.at[dst : dst + n],
            send_sem=y_send.at[chunk, side], recv_sem=y_recv.at[chunk, 1 - side],
            device_id=frames[side][1], device_id_type=MESH,
        )

    def y_start(chunk):
        for side in range(2):
            when(frames[side][0], lambda side=side: y_copy(chunk, side).start())

    def y_arrived(chunk, slot):
        start, n = CHUNKS[chunk]
        dst = (C1, C2, C3)[chunk][slot]
        return pltpu.make_async_remote_copy(
            src_ref=xs.at[dst : dst + n], dst_ref=xs.at[dst : dst + n],
            send_sem=y_send.at[chunk, slot], recv_sem=y_recv.at[chunk, slot],
            device_id=frames[slot][1], device_id_type=MESH,
        )

    def h_copy(slot, d):
        off, n = PIECES[opposite[d]]
        dst = HALO_AT[slot] + off
        if d < 2:
            base = (OWN, C1[0], C1[1])[slot] + 48 * d
            src = xs.at[base : base + 48]
        else:
            so = PIECES[d][0] - 96
            src = packed.at[slot, so : so + n]
        return pltpu.make_async_remote_copy(
            src_ref=src, dst_ref=xs.at[dst : dst + n],
            send_sem=h_send.at[slot, d], recv_sem=h_recv.at[slot, opposite[d]],
            device_id=dirs[d][1], device_id_type=MESH,
        )

    def h_arrived(slot, d):
        off, n = PIECES[d]
        dst = HALO_AT[slot] + off
        return pltpu.make_async_remote_copy(
            src_ref=xs.at[dst : dst + n], dst_ref=xs.at[dst : dst + n],
            send_sem=h_send.at[slot, d], recv_sem=h_recv.at[slot, d],
            device_id=dirs[d][1], device_id_type=MESH,
        )

    def h_start(slot, which):
        for d in which:
            when(dirs[d][0], lambda d=d: h_copy(slot, d).start())

    def h_wait(slot, which):
        for d in which:
            when(dirs[d][0], lambda d=d: h_arrived(slot, d).wait_recv())

    def pack(slot):
        if slot == 0:
            edge = xs[0:160, :]
        else:
            b, c = C1[slot - 1], C2[slot - 1]
            edge = jnp.concatenate([xs[b : b + 96, :], xs[c : c + 64, :]], axis=0)
        packed[slot] = jnp.dot(pack_ref[...], edge, preferred_element_type=F32).astype(BF)

    y_start(0)
    h_start(0, (0, 1))
    y_start(1)
    pack(0)
    h_start(0, range(2, 8))
    y_start(2)

    def clear(start, n):
        xs[start : start + n, :] = jnp.zeros((n, D), BF)

    for slot in range(2):
        def absent(slot=slot):
            for (_, n), c in zip(CHUNKS, (C1, C2, C3)):
                clear(c[slot], n)
            clear(HALOS[slot], 256)
        pl.when(jnp.logical_not(frames[slot][0]))(absent)
    for cond, pieces in ((has_north, (2, 4, 5)), (has_south, (3, 6, 7))):
        def edge_clear(pieces=pieces):
            for slot in range(3):
                present = None if slot == 0 else frames[slot - 1][0]
                for d in pieces:
                    off, n = PIECES[d]
                    when(present, lambda off=off, n=n, slot=slot: clear(HALO_AT[slot] + off, n))
        pl.when(jnp.logical_not(cond))(edge_clear)

    j = lax.broadcasted_iota(jnp.int32, (1, KEYS), 1)
    extra = jnp.zeros((1, KEYS), F32)

    def bar(extra, cond, start, n):
        off = (j >= start) & (j < start + n) & jnp.logical_not(cond)
        return jnp.where(off, MASKED, extra)

    for slot in range(2):
        for (_, n), c in zip(CHUNKS, (C1, C2, C3)):
            extra = bar(extra, frames[slot][0], c[slot], n)
        extra = bar(extra, frames[slot][0], HALOS[slot], 256)
    for base in HALO_AT:
        for cond, pieces in ((has_north, (2, 4, 5)), (has_south, (3, 6, 7))):
            for d in pieces:
                extra = bar(extra, cond, base + PIECES[d][0], PIECES[d][1])
    bias[...] = jnp.minimum(bias_ref[...].astype(F32), extra)

    def rms(p, gain):
        ms = jnp.mean(p * p, axis=-1, keepdims=True)
        return (p * lax.rsqrt(ms + 1e-06) * gain).astype(BF)

    def keys_of(start, n):
        p = jnp.dot(xs[start : start + n, :], wk[...], preferred_element_type=F32)
        ks[start : start + n, :] = rms(p, kgain_ref[...])

    def values_of(start, n):
        vs[start : start + n, :] = jnp.dot(
            xs[start : start + n, :], wv[...], preferred_element_type=F32
        ).astype(BF)

    def attend(start, n, first):
        @pl.loop(0, HEADS)
        def _(h):
            hs = pl.ds(pl.multiple_of(h * HEAD_DIM, HEAD_DIM), HEAD_DIM)
            s = lax.dot_general(
                qs[:, hs], ks[start : start + n, hs], (((1,), (1,)), ((), ())), preferred_element_type=F32
            )
            s = s * SCALE + bias[:, start : start + n]
            m = jnp.max(s, axis=-1, keepdims=True)
            if not first:
                old = m_ref[h]
                m = jnp.maximum(m, old)
            p = jnp.exp2(s - m)
            l = jnp.sum(p, axis=-1, keepdims=True)
            pv = jnp.dot(p.astype(BF), vs[start : start + n, hs], preferred_element_type=F32)
            if not first:
                alpha = jnp.exp2(old - m)
                l = l + alpha * l_ref[h]
                pv = pv + alpha * acc[:, hs]
            m_ref[h] = m
            l_ref[h] = l
            acc[:, hs] = pv

    loads[0].wait()
    qs[...] = rms(jnp.dot(xs[0:TOKENS, :], wq[...], preferred_element_type=F32), qgain_ref[...])
    loads[1].wait()
    keys_of(0, TOKENS)
    loads[2].wait()
    values_of(0, TOKENS)

    for slot in range(2):
        def forward(slot=slot):
            y_arrived(0, slot).wait_recv()
            h_start(slot + 1, (0, 1))
        pl.when(frames[slot][0])(forward)
    h_wait(0, range(8))
    keys_of(256, 448)
    for slot in range(2):
        def forward(slot=slot):
            y_arrived(1, slot).wait_recv()
            pack(slot + 1)
            h_start(slot + 1, range(2, 8))
        pl.when(frames[slot][0])(forward)
    values_of(256, 448)
    attend(0, 512, True)
    for slot in range(2):
        pl.when(frames[slot][0])(lambda slot=slot: y_arrived(2, slot).wait_recv())
    pl.when(has_prev)(lambda: h_wait(1, range(8)))
    keys_of(704, 576)
    values_of(704, 576)
    attend(512, 768, False)
    pl.when(has_next)(lambda: h_wait(2, range(8)))
    keys_of(1280, 256)
    values_of(1280, 256)
    attend(1280, 256, False)

    @pl.loop(0, HEADS)
    def _(h):
        hs = pl.ds(pl.multiple_of(h * HEAD_DIM, HEAD_DIM), HEAD_DIM)
        qs[:, hs] = (acc[:, hs] / l_ref[h]).astype(BF)

    flat[...] = jnp.dot(back_ref[...], qs[...], preferred_element_type=F32).astype(BF)
    loads[3].wait()
    out_ref[...] = (jnp.dot(flat[...], wo[...], preferred_element_type=F32) * gate_ref[...]).astype(BF)

    for chunk in range(3):
        for side in range(2):
            when(frames[side][0], lambda chunk=chunk, side=side: y_copy(chunk, side).wait_send())
    for slot in range(3):
        present = None if slot == 0 else frames[slot - 1][0]
        for d in range(8):
            def done(slot=slot, d=d):
                when(dirs[d][0], lambda: h_copy(slot, d).wait_send())
            when(present, done)


def shards(latents, ada_shift, ada_scale, ada_gate, w_query, w_key, w_value, w_out, query_gain, key_gain):
    perm, back, pack, bias = tables()
    row = lambda v: v.reshape(1, D)
    vmem = pl.BlockSpec(memory_space=pltpu.VMEM)
    hbm = pl.BlockSpec(memory_space=pl.ANY)
    out = pl.pallas_call(
        kernel,
        out_shape=jax.ShapeDtypeStruct((TOKENS, D), BF),
        in_specs=[vmem] * 6 + [hbm] * 4 + [vmem] * 4,
        out_specs=vmem,
        scratch_shapes=[pltpu.VMEM((D, D), BF)] * 4
        + [
            pltpu.VMEM((KEYS, D), BF),
            pltpu.VMEM((KEYS, D), BF),
            pltpu.VMEM((KEYS, D), BF),
            pltpu.VMEM((TOKENS, D), BF),
            pltpu.VMEM((3, 160, D), BF),
            pltpu.VMEM((TOKENS, D), BF),
            pltpu.VMEM((TOKENS, KEYS), F32),
            pltpu.VMEM((TOKENS, D), F32),
            pltpu.VMEM((HEADS, TOKENS, 1), F32),
            pltpu.VMEM((HEADS, TOKENS, 1), F32),
            pltpu.SemaphoreType.DMA((4,)),
            pltpu.SemaphoreType.DMA((3, 2)),
            pltpu.SemaphoreType.DMA((3, 2)),
            pltpu.SemaphoreType.DMA((3, 8)),
            pltpu.SemaphoreType.DMA((3, 8)),
        ],
        compiler_params=pltpu.CompilerParams(
            collective_id=0, has_side_effects=True, vmem_limit_bytes=60 * 2**20
        ),
        cost_estimate=pl.CostEstimate(flops=2 * 10**10, bytes_accessed=2 * 10**7, transcendentals=5 * 10**6),
    )(
        latents.reshape(TOKENS, D), row(ada_shift), row(ada_scale), row(ada_gate), row(query_gain), row(key_gain),
        w_query, w_key, w_value, w_out,
        jnp.asarray(perm, BF), jnp.asarray(back, BF), jnp.asarray(pack, BF), jnp.asarray(bias, BF),
    )
    return out.reshape(latents.shape)


def solution(mesh):
    return jax.shard_map(
        shards,
        mesh=mesh,
        in_specs=(P("tm", "lat", "lon", None),) + (P(),) * 9,
        out_specs=P("tm", "lat", "lon", None),
        check_vma=False,
    )
```

```python
import functools
import math

import jax
import jax.numpy as jnp
import numpy as np
from jax import lax
from jax.experimental import pallas as pl
from jax.experimental.pallas import tpu as pltpu
from jax.sharding import PartitionSpec as P

HEADS = 12
HEAD_DIM = 128
D = 1536
SIDE = 16
TOKENS = SIDE * SIDE
KEYS = 1536
BF = jnp.bfloat16
F32 = jnp.float32
MESH = pl.DeviceIdType.MESH
MASKED = -1e30
GROUP = 4
SCALE = HEAD_DIM ** (-0.5) * math.log2(math.e)

CHUNKS = ((0, 48), (48, 112), None, (160, 96))
CHUNK_ROWS = (48, 112, 48, 96)
CHUNK_AT = ((512, 560), (608, 720), (832, 880), (1024, 1120))
HALO_E = 304
WEST_AT = (256, 928, 976)
ROWS_AT = (352, 1216, 1376)


def center_order():
    order = [(r, c) for c in (13, 14, 15, 0, 1, 2) for r in range(16)]
    order += [(r, c) for r in (0, 1, 2) for c in range(3, 13)]
    order += [(r, c) for r in (13, 14, 15) for c in range(3, 13)]
    order += [(r, c) for r in range(3, 13) for c in range(3, 13)]
    return order


def tables():
    order = center_order()
    natural = [(r, c) for r in range(SIDE) for c in range(SIDE)]
    west = [(r, c - 16) for c in (13, 14, 15) for r in range(16)]
    east = [(r, c + 16) for c in (0, 1, 2) for r in range(16)]
    bands = [[(r, c) for r in rows for c in range(-3, 19)] + [None] * 14 for rows in ((0, 1, 2), (13, 14, 15))]
    north = [p and (p[0] - 16, p[1]) for p in bands[1]]
    south = [p and (p[0] + 16, p[1]) for p in bands[0]]
    select = np.zeros((TOKENS, TOKENS), np.float32)
    for i, (r, c) in enumerate(order):
        select[i, r * SIDE + c] = 1
    where = {p: i for i, p in enumerate(order[:160] + west + east)}
    pack = np.zeros((160, 256), np.float32)
    for i, p in enumerate(bands[0] + bands[1]):
        if p is not None:
            pack[i, where[p]] = 1
    keys = [None] * KEYS

    def place(start, cells):
        keys[start : start + len(cells)] = cells

    place(0, natural)
    place(HALO_E, east)
    for chunk, spots in zip(CHUNKS, CHUNK_AT):
        for spot in spots:
            place(spot, order[chunk[0] : sum(chunk)] if chunk else east)
    for slot in range(3):
        place(WEST_AT[slot], west)
        place(ROWS_AT[slot], north + south)
    bias = np.full((TOKENS, KEYS), MASKED, np.float32)
    for j, p in enumerate(keys):
        if p is None:
            continue
        for i, (r, c) in enumerate(natural):
            if abs(r - p[0]) <= 3 and abs(c - p[1]) <= 3:
                bias[i, j] = 0
    return select, pack, bias


def kernel(
    x_ref, shift_ref, scale_ref, gate_ref, qgain_ref, kgain_ref, wq_any, wk_any, wv_any, wo_any,
    select_ref, pack_ref, bias_any, out_ref,
    wq, wk, wv, wo, xs, ks, vs, qs, staged, packed, bias_in, bias, acc, m_ref, l_ref, score, prob, new_m, new_l,
    w_sem, y_send, y_recv, h_send, h_recv,
):
    t, a, o = lax.axis_index("tm"), lax.axis_index("lat"), lax.axis_index("lon")
    west, east = lax.rem(o + 7, 8), lax.rem(o + 1, 8)
    has_prev, has_next = t > 0, t < 3
    has_north, has_south = a > 0, a < 3
    dirs = (
        (None, (t, a, west)), (None, (t, a, east)),
        (has_north, (t, a - 1, o)), (has_south, (t, a + 1, o)),
    )
    opposite = (1, 0, 3, 2)
    frames = ((has_prev, (t - 1, a, o)), (has_next, (t + 1, a, o)))

    def when(cond, fn):
        if cond is None:
            fn()
        else:
            pl.when(cond)(fn)

    loads = []
    pairs = ((wq_any, wq), (wk_any, wk), (bias_any, bias_in), (wv_any, wv), (wo_any, wo))
    for i, (src, dst) in enumerate(pairs):
        loads.append(pltpu.make_async_copy(src, dst, w_sem.at[i]))
        loads[-1].start()

    barrier = pltpu.get_barrier_semaphore()
    for cond, dev in dirs + frames:
        when(cond, lambda dev=dev: pl.semaphore_signal(barrier, inc=1, device_id=dev, device_id_type=MESH))

    one = lambda c: jnp.where(c, 1, 0)

    row = lambda ref: ref[...].reshape(1, D)
    shift, scale = row(shift_ref), 1.0 + row(scale_ref)

    @pl.loop(0, 8)
    def _(i):
        rows = pl.ds(pl.multiple_of(i * 32, 32), 32)
        v = x_ref[rows, :].astype(F32)
        centred = v - jnp.mean(v, axis=-1, keepdims=True)
        var = jnp.mean(centred * centred, axis=-1, keepdims=True)
        xs[rows, :] = (centred * lax.rsqrt(var + 1e-06) * scale + shift).astype(BF)

    staged[...] = jnp.dot(select_ref[...], xs[0:TOKENS, :], preferred_element_type=F32).astype(BF)
    pl.semaphore_wait(barrier, 2 + one(has_prev) + one(has_next) + one(has_north) + one(has_south))

    def y_copy(chunk, side):
        n, dst = CHUNK_ROWS[chunk], CHUNK_AT[chunk][1 - side]
        if CHUNKS[chunk]:
            src = staged.at[CHUNKS[chunk][0] : sum(CHUNKS[chunk])]
        else:
            src = xs.at[HALO_E : HALO_E + n]
        return pltpu.make_async_remote_copy(
            src_ref=src, dst_ref=xs.at[dst : dst + n],
            send_sem=y_send.at[chunk, side], recv_sem=y_recv.at[chunk, 1 - side],
            device_id=frames[side][1], device_id_type=MESH,
        )

    def y_start(chunk):
        for side in range(2):
            when(frames[side][0], lambda side=side: y_copy(chunk, side).start())

    def y_arrived(chunk, slot):
        n, dst = CHUNK_ROWS[chunk], CHUNK_AT[chunk][slot]
        return pltpu.make_async_remote_copy(
            src_ref=xs.at[dst : dst + n], dst_ref=xs.at[dst : dst + n],
            send_sem=y_send.at[chunk, slot], recv_sem=y_recv.at[chunk, slot],
            device_id=frames[slot][1], device_id_type=MESH,
        )

    def piece(slot, d):
        if d == 0:
            return WEST_AT[slot], 48
        if d == 1:
            return HALO_E, 48
        return ROWS_AT[slot] + 80 * (d - 2), 80

    def h_copy(slot, d):
        dst, n = piece(slot, opposite[d])
        if d >= 2:
            src = packed.at[slot, 80 * (d - 2) : 80 * (d - 1)]
        elif slot == 0:
            src = staged.at[48 - 48 * d : 96 - 48 * d]
        else:
            src = xs.at[CHUNK_AT[0][slot - 1] : CHUNK_AT[0][slot - 1] + 48]
        return pltpu.make_async_remote_copy(
            src_ref=src, dst_ref=xs.at[dst : dst + n],
            send_sem=h_send.at[slot, d], recv_sem=h_recv.at[slot, opposite[d]],
            device_id=dirs[d][1], device_id_type=MESH,
        )

    def h_arrived(slot, d):
        dst, n = piece(slot, d)
        return pltpu.make_async_remote_copy(
            src_ref=xs.at[dst : dst + n], dst_ref=xs.at[dst : dst + n],
            send_sem=h_send.at[slot, d], recv_sem=h_recv.at[slot, d],
            device_id=dirs[d][1], device_id_type=MESH,
        )

    def h_start(slot, which):
        for d in which:
            when(dirs[d][0], lambda d=d: h_copy(slot, d).start())

    def h_wait(slot, which):
        for d in which:
            when(dirs[d][0], lambda d=d: h_arrived(slot, d).wait_recv())

    def y_sent(chunk):
        for side in range(2):
            when(frames[side][0], lambda side=side: y_copy(chunk, side).wait_send())

    def h_sent(slot, which):
        for d in which:
            when(dirs[d][0], lambda d=d: h_copy(slot, d).wait_send())

    def pack(slot):
        if slot == 0:
            parts = [staged[0:160, :], xs[256:352, :]]
        else:
            spots = [(CHUNK_AT[k][slot - 1], CHUNK_ROWS[k]) for k in range(3)]
            spots.insert(2, (WEST_AT[slot], 48))
            parts = [xs[p : p + n, :] for p, n in spots]
        edge = jnp.concatenate(parts, axis=0)
        packed[slot] = jnp.dot(pack_ref[...], edge, preferred_element_type=F32).astype(BF)

    y_start(0)
    h_start(0, (0, 1))

    def clear(start, n):
        xs[start : start + n, :] = jnp.zeros((n, D), BF)

    for slot in range(2):
        def absent(slot=slot):
            for n, c in zip(CHUNK_ROWS, CHUNK_AT):
                clear(c[slot], n)
            clear(WEST_AT[slot + 1], 48)
            clear(ROWS_AT[slot + 1], 160)
        pl.when(jnp.logical_not(frames[slot][0]))(absent)
    for d in (2, 3):
        def edge_clear(d=d):
            for slot in range(3):
                present = None if slot == 0 else frames[slot - 1][0]
                start, n = piece(slot, d)
                when(present, lambda start=start, n=n: clear(start, n))
        pl.when(jnp.logical_not(dirs[d][0]))(edge_clear)

    j = lax.broadcasted_iota(jnp.int32, (1, KEYS), 1)
    extra = jnp.zeros((1, KEYS), F32)

    def bar(extra, cond, start, n):
        off = (j >= start) & (j < start + n) & jnp.logical_not(cond)
        return jnp.where(off, MASKED, extra)

    for slot in range(2):
        for n, c in zip(CHUNK_ROWS, CHUNK_AT):
            extra = bar(extra, frames[slot][0], c[slot], n)
        extra = bar(extra, frames[slot][0], WEST_AT[slot + 1], 48)
        extra = bar(extra, frames[slot][0], ROWS_AT[slot + 1], 160)
    for slot in range(3):
        for d in (2, 3):
            extra = bar(extra, dirs[d][0], *piece(slot, d))

    def rms(p, gain):
        ms = jnp.mean(p * p, axis=-1, keepdims=True)
        return (p * lax.rsqrt(ms + 1e-06) * gain).astype(BF)

    def keys_of(start, n):
        p = jnp.dot(xs[start : start + n, :], wk[...], preferred_element_type=F32)
        ks[start : start + n, :] = rms(p, row(kgain_ref))

    def values_of(start, n):
        vs[start : start + n, :] = jnp.dot(
            xs[start : start + n, :], wv[...], preferred_element_type=F32
        ).astype(BF)

    def attend(start, n, first, last):
        @pl.loop(0, HEADS // GROUP)
        def _(g):
            heads = [g * GROUP + u for u in range(GROUP)]
            at = [pl.ds(pl.multiple_of(h * HEAD_DIM, HEAD_DIM), HEAD_DIM) for h in heads]
            for u in range(GROUP):
                score[u, :, 0:n] = lax.dot_general(
                    qs[:, at[u]], ks[start : start + n, at[u]], (((1,), (1,)), ((), ())), preferred_element_type=F32
                )
            for u in range(GROUP):
                for r in range(0, TOKENS, 16):
                    rs = slice(r, r + 16)
                    s = score[u, rs, 0:n] * SCALE + bias[rs, start : start + n].astype(F32)
                    m = jnp.max(s, axis=-1, keepdims=True)
                    p = jnp.exp2(s - m)
                    new_m[u, rs] = jnp.broadcast_to(m, (16, HEAD_DIM))
                    new_l[u, rs] = jnp.broadcast_to(jnp.sum(p, axis=-1, keepdims=True), (16, HEAD_DIM))
                    prob[u, rs, 0:n] = p.astype(BF)
                pv = jnp.dot(prob[u, :, 0:n], vs[start : start + n, at[u]], preferred_element_type=F32)
                if first:
                    acc[:, at[u]] = pv
                    m_ref[heads[u]] = new_m[u]
                    l_ref[heads[u]] = new_l[u]
                else:
                    m1, m2 = m_ref[heads[u]], new_m[u]
                    m = jnp.maximum(m1, m2)
                    a1, a2 = jnp.exp2(m1 - m), jnp.exp2(m2 - m)
                    total = a1 * l_ref[heads[u]] + a2 * new_l[u]
                    joined = a1 * acc[:, at[u]] + a2 * pv
                    if last:
                        qs[:, at[u]] = (joined / total).astype(BF)
                    else:
                        acc[:, at[u]] = joined
                        m_ref[heads[u]] = m
                        l_ref[heads[u]] = total

    def each(fn, slots=(0, 1)):
        for slot in slots:
            pl.when(frames[slot][0])(functools.partial(fn, slot))

    loads[0].wait()
    qs[...] = rms(jnp.dot(xs[0:TOKENS, :], wq[...], preferred_element_type=F32), row(qgain_ref))
    loads[1].wait()
    keys_of(0, 256)
    loads[2].wait()
    bias[...] = jnp.minimum(bias_in[...].astype(F32), extra).astype(BF)
    loads[3].wait()
    values_of(0, 256)

    y_sent(0)
    y_start(1)

    def columns_on(slot):
        y_arrived(0, slot).wait_recv()
        h_start(slot + 1, (1,))

    each(columns_on)
    h_wait(0, (0, 1))
    y_start(2)
    pack(0)
    h_start(0, (2, 3))
    keys_of(256, 96)
    values_of(256, 96)
    keys_of(512, 96)
    values_of(512, 96)
    h_wait(0, (2, 3))
    keys_of(352, 160)
    values_of(352, 160)
    y_start(3)
    attend(0, 512, True, False)

    def rows_on(slot):
        y_arrived(1, slot).wait_recv()
        y_arrived(2, slot).wait_recv()
        h_wait(slot + 1, (0,))
        pack(slot + 1)
        h_start(slot + 1, (2, 3))

    each(rows_on)
    keys_of(608, 416)
    values_of(608, 416)
    attend(512, 512, False, False)
    each(lambda slot: y_arrived(3, slot).wait_recv())
    each(lambda slot: h_wait(slot + 1, (2, 3)))
    keys_of(1024, 512)
    values_of(1024, 512)
    attend(1024, 512, False, True)

    loads[4].wait()
    out_ref[...] = (jnp.dot(qs[...], wo[...], preferred_element_type=F32) * row(gate_ref)).astype(BF)

    for chunk in (1, 2, 3):
        y_sent(chunk)
    h_sent(0, range(4))
    each(lambda slot: h_sent(slot + 1, (1, 2, 3)))


def shards(latents, ada_shift, ada_scale, ada_gate, w_query, w_key, w_value, w_out, query_gain, key_gain):
    select, pack, bias = tables()
    vmem = pl.BlockSpec(memory_space=pltpu.VMEM)
    hbm = pl.BlockSpec(memory_space=pl.ANY)
    out = pl.pallas_call(
        kernel,
        out_shape=jax.ShapeDtypeStruct((TOKENS, D), BF),
        in_specs=[vmem] * 6 + [hbm] * 4 + [vmem] * 2 + [hbm],
        out_specs=vmem,
        scratch_shapes=[pltpu.VMEM((D, D), BF)] * 4
        + [
            pltpu.VMEM((KEYS, D), BF),
            pltpu.VMEM((KEYS, D), BF),
            pltpu.VMEM((KEYS, D), BF),
            pltpu.VMEM((TOKENS, D), BF),
            pltpu.VMEM((TOKENS, D), BF),
            pltpu.VMEM((3, 160, D), BF),
            pltpu.VMEM((TOKENS, KEYS), BF),
            pltpu.VMEM((TOKENS, KEYS), BF),
            pltpu.VMEM((TOKENS, D), F32),
            pltpu.VMEM((HEADS, TOKENS, HEAD_DIM), F32),
            pltpu.VMEM((HEADS, TOKENS, HEAD_DIM), F32),
            pltpu.VMEM((GROUP, TOKENS, 512), F32),
            pltpu.VMEM((GROUP, TOKENS, 512), BF),
            pltpu.VMEM((GROUP, TOKENS, HEAD_DIM), F32),
            pltpu.VMEM((GROUP, TOKENS, HEAD_DIM), F32),
            pltpu.SemaphoreType.DMA((5,)),
            pltpu.SemaphoreType.DMA((4, 2)),
            pltpu.SemaphoreType.DMA((4, 2)),
            pltpu.SemaphoreType.DMA((3, 4)),
            pltpu.SemaphoreType.DMA((3, 4)),
        ],
        compiler_params=pltpu.CompilerParams(
            collective_id=0, has_side_effects=True, vmem_limit_bytes=62 * 2**20
        ),
        cost_estimate=pl.CostEstimate(flops=2 * 10**10, bytes_accessed=2 * 10**7, transcendentals=5 * 10**6),
    )(
        latents.reshape(TOKENS, D), ada_shift, ada_scale, ada_gate, query_gain, key_gain,
        w_query, w_key, w_value, w_out,
        jnp.asarray(select, BF), jnp.asarray(pack, BF), jnp.asarray(bias, BF),
    )
    return out.reshape(latents.shape)


def solution(mesh):
    return jax.shard_map(
        shards,
        mesh=mesh,
        in_specs=(P("tm", "lat", "lon", None),) + (P(),) * 9,
        out_specs=P("tm", "lat", "lon", None),
        check_vma=False,
    )
```

```python
import functools
import math

import jax
import jax.numpy as jnp
import numpy as np
from jax import lax
from jax.experimental import pallas as pl
from jax.experimental.pallas import tpu as pltpu
from jax.sharding import PartitionSpec as P

HEADS = 12
HEAD_DIM = 128
D = 1536
SIDE = 16
TOKENS = SIDE * SIDE
KEYS = 1536
BF = jnp.bfloat16
F32 = jnp.float32
MESH = pl.DeviceIdType.MESH
MASKED = -1e30
GROUP = 4
SCALE = HEAD_DIM ** (-0.5) * math.log2(math.e)

CHUNKS = ((0, 48), (48, 112), None, (160, 96))
CHUNK_ROWS = (48, 112, 48, 96)
CHUNK_AT = ((352, 400), (448, 560), (672, 720), (1024, 1120))
HALO_E = 304
WEST_AT = (256, 768, 816)
ROWS_AT = (864, 1216, 1376)


def center_order():
    order = [(r, c) for c in (13, 14, 15, 0, 1, 2) for r in range(16)]
    order += [(r, c) for r in (0, 1, 2) for c in range(3, 13)]
    order += [(r, c) for r in (13, 14, 15) for c in range(3, 13)]
    order += [(r, c) for r in range(3, 13) for c in range(3, 13)]
    return order


def tables():
    order = center_order()
    natural = [(r, c) for r in range(SIDE) for c in range(SIDE)]
    west = [(r, c - 16) for c in (13, 14, 15) for r in range(16)]
    east = [(r, c + 16) for c in (0, 1, 2) for r in range(16)]
    bands = [[(r, c) for r in rows for c in range(-3, 19)] + [None] * 14 for rows in ((0, 1, 2), (13, 14, 15))]
    north = [p and (p[0] - 16, p[1]) for p in bands[1]]
    south = [p and (p[0] + 16, p[1]) for p in bands[0]]
    select = np.zeros((TOKENS, TOKENS), np.float32)
    for i, (r, c) in enumerate(order):
        select[i, r * SIDE + c] = 1
    where = {p: i for i, p in enumerate(order[:160] + west + east)}
    pack = np.zeros((160, 256), np.float32)
    for i, p in enumerate(bands[0] + bands[1]):
        if p is not None:
            pack[i, where[p]] = 1
    keys = [None] * KEYS

    def place(start, cells):
        keys[start : start + len(cells)] = cells

    place(0, natural)
    place(HALO_E, east)
    for chunk, spots in zip(CHUNKS, CHUNK_AT):
        for spot in spots:
            place(spot, order[chunk[0] : sum(chunk)] if chunk else east)
    for slot in range(3):
        place(WEST_AT[slot], west)
        place(ROWS_AT[slot], north + south)
    bias = np.full((TOKENS, KEYS), MASKED, np.float32)
    for j, p in enumerate(keys):
        if p is None:
            continue
        for i, (r, c) in enumerate(natural):
            if abs(r - p[0]) <= 3 and abs(c - p[1]) <= 3:
                bias[i, j] = 0
    return select, pack, bias


def kernel(
    x_ref, shift_ref, scale_ref, gate_ref, qgain_ref, kgain_ref, wq_any, wk_any, wv_any, wo_any,
    select_ref, pack_ref, bias_any, out_any,
    wq, wk, wv, wo, xs, ks, vs, qs, staged, packed, bias_in, bias, acc, m_ref, l_ref, score, prob, new_m, new_l,
    w_sem, o_sem, y_send, y_recv, h_send, h_recv,
):
    t, a, o = lax.axis_index("tm"), lax.axis_index("lat"), lax.axis_index("lon")
    west, east = lax.rem(o + 7, 8), lax.rem(o + 1, 8)
    has_prev, has_next = t > 0, t < 3
    has_north, has_south = a > 0, a < 3
    dirs = (
        (None, (t, a, west)), (None, (t, a, east)),
        (has_north, (t, a - 1, o)), (has_south, (t, a + 1, o)),
    )
    opposite = (1, 0, 3, 2)
    frames = ((has_prev, (t - 1, a, o)), (has_next, (t + 1, a, o)))

    def when(cond, fn):
        if cond is None:
            fn()
        else:
            pl.when(cond)(fn)

    loads = []
    pairs = ((wq_any, wq), (wk_any, wk), (bias_any, bias_in), (wv_any, wv), (wo_any, wo))
    for i, (src, dst) in enumerate(pairs):
        loads.append(pltpu.make_async_copy(src, dst, w_sem.at[i]))
        loads[-1].start()

    barrier = pltpu.get_barrier_semaphore()
    for cond, dev in dirs + frames:
        when(cond, lambda dev=dev: pl.semaphore_signal(barrier, inc=1, device_id=dev, device_id_type=MESH))

    one = lambda c: jnp.where(c, 1, 0)

    row = lambda ref: ref[...].reshape(1, D)
    shift, scale = row(shift_ref), 1.0 + row(scale_ref)

    @pl.loop(0, 8)
    def _(i):
        rows = pl.ds(pl.multiple_of(i * 32, 32), 32)
        v = x_ref[rows, :].astype(F32)
        centred = v - jnp.mean(v, axis=-1, keepdims=True)
        var = jnp.mean(centred * centred, axis=-1, keepdims=True)
        xs[rows, :] = (centred * lax.rsqrt(var + 1e-06) * scale + shift).astype(BF)

    staged[...] = jnp.dot(select_ref[...], xs[0:TOKENS, :], preferred_element_type=F32).astype(BF)
    pl.semaphore_wait(barrier, 2 + one(has_prev) + one(has_next) + one(has_north) + one(has_south))

    def y_copy(chunk, side):
        n, dst = CHUNK_ROWS[chunk], CHUNK_AT[chunk][1 - side]
        if CHUNKS[chunk]:
            src = staged.at[CHUNKS[chunk][0] : sum(CHUNKS[chunk])]
        else:
            src = xs.at[HALO_E : HALO_E + n]
        return pltpu.make_async_remote_copy(
            src_ref=src, dst_ref=xs.at[dst : dst + n],
            send_sem=y_send.at[chunk, side], recv_sem=y_recv.at[chunk, 1 - side],
            device_id=frames[side][1], device_id_type=MESH,
        )

    def y_start(chunk):
        for side in range(2):
            when(frames[side][0], lambda side=side: y_copy(chunk, side).start())

    def y_arrived(chunk, slot):
        n, dst = CHUNK_ROWS[chunk], CHUNK_AT[chunk][slot]
        return pltpu.make_async_remote_copy(
            src_ref=xs.at[dst : dst + n], dst_ref=xs.at[dst : dst + n],
            send_sem=y_send.at[chunk, slot], recv_sem=y_recv.at[chunk, slot],
            device_id=frames[slot][1], device_id_type=MESH,
        )

    def piece(slot, d):
        if d == 0:
            return WEST_AT[slot], 48
        if d == 1:
            return HALO_E, 48
        return ROWS_AT[slot] + 80 * (d - 2), 80

    def h_copy(slot, d):
        dst, n = piece(slot, opposite[d])
        if d >= 2:
            src = packed.at[slot, 80 * (d - 2) : 80 * (d - 1)]
        elif slot == 0:
            src = staged.at[48 - 48 * d : 96 - 48 * d]
        else:
            src = xs.at[CHUNK_AT[0][slot - 1] : CHUNK_AT[0][slot - 1] + 48]
        return pltpu.make_async_remote_copy(
            src_ref=src, dst_ref=xs.at[dst : dst + n],
            send_sem=h_send.at[slot, d], recv_sem=h_recv.at[slot, opposite[d]],
            device_id=dirs[d][1], device_id_type=MESH,
        )

    def h_arrived(slot, d):
        dst, n = piece(slot, d)
        return pltpu.make_async_remote_copy(
            src_ref=xs.at[dst : dst + n], dst_ref=xs.at[dst : dst + n],
            send_sem=h_send.at[slot, d], recv_sem=h_recv.at[slot, d],
            device_id=dirs[d][1], device_id_type=MESH,
        )

    def h_start(slot, which):
        for d in which:
            when(dirs[d][0], lambda d=d: h_copy(slot, d).start())

    def h_wait(slot, which):
        for d in which:
            when(dirs[d][0], lambda d=d: h_arrived(slot, d).wait_recv())

    def y_sent(chunk):
        for side in range(2):
            when(frames[side][0], lambda side=side: y_copy(chunk, side).wait_send())

    def h_sent(slot, which):
        for d in which:
            when(dirs[d][0], lambda d=d: h_copy(slot, d).wait_send())

    def pack(slot):
        if slot == 0:
            parts = [staged[0:160, :], xs[256:352, :]]
        else:
            spots = [(CHUNK_AT[k][slot - 1], CHUNK_ROWS[k]) for k in range(3)]
            spots.insert(2, (WEST_AT[slot], 48))
            parts = [xs[p : p + n, :] for p, n in spots]
        edge = jnp.concatenate(parts, axis=0)
        packed[slot] = jnp.dot(pack_ref[...], edge, preferred_element_type=F32).astype(BF)

    y_start(0)
    h_start(0, (0, 1))

    def clear(start, n):
        xs[start : start + n, :] = jnp.zeros((n, D), BF)

    for slot in range(2):
        def absent(slot=slot):
            for n, c in zip(CHUNK_ROWS, CHUNK_AT):
                clear(c[slot], n)
            clear(WEST_AT[slot + 1], 48)
            clear(ROWS_AT[slot + 1], 160)
        pl.when(jnp.logical_not(frames[slot][0]))(absent)
    for d in (2, 3):
        def edge_clear(d=d):
            for slot in range(3):
                present = None if slot == 0 else frames[slot - 1][0]
                start, n = piece(slot, d)
                when(present, lambda start=start, n=n: clear(start, n))
        pl.when(jnp.logical_not(dirs[d][0]))(edge_clear)

    j = lax.broadcasted_iota(jnp.int32, (1, KEYS), 1)
    extra = jnp.zeros((1, KEYS), F32)

    def bar(extra, cond, start, n):
        off = (j >= start) & (j < start + n) & jnp.logical_not(cond)
        return jnp.where(off, MASKED, extra)

    for slot in range(2):
        for n, c in zip(CHUNK_ROWS, CHUNK_AT):
            extra = bar(extra, frames[slot][0], c[slot], n)
        extra = bar(extra, frames[slot][0], WEST_AT[slot + 1], 48)
        extra = bar(extra, frames[slot][0], ROWS_AT[slot + 1], 160)
    for slot in range(3):
        for d in (2, 3):
            extra = bar(extra, dirs[d][0], *piece(slot, d))

    def rms(p, gain):
        ms = jnp.mean(p * p, axis=-1, keepdims=True)
        return (p * lax.rsqrt(ms + 1e-06) * gain).astype(BF)

    def keys_of(start, n):
        p = jnp.dot(xs[start : start + n, :], wk[...], preferred_element_type=F32)
        ks[start : start + n, :] = rms(p, row(kgain_ref))

    def values_of(start, n):
        vs[start : start + n, :] = jnp.dot(
            xs[start : start + n, :], wv[...], preferred_element_type=F32
        ).astype(BF)

    def attend(start, n, first, last):
        @pl.loop(0, HEADS // GROUP)
        def _(g):
            heads = [g * GROUP + u for u in range(GROUP)]
            at = [pl.ds(pl.multiple_of(h * HEAD_DIM, HEAD_DIM), HEAD_DIM) for h in heads]
            for u in range(GROUP):
                score[u, :, 0:n] = lax.dot_general(
                    qs[:, at[u]], ks[start : start + n, at[u]], (((1,), (1,)), ((), ())), preferred_element_type=F32
                )
            for u in range(GROUP):
                for r in range(0, TOKENS, 16):
                    rs = slice(r, r + 16)
                    s = score[u, rs, 0:n] * SCALE + bias[rs, start : start + n].astype(F32)
                    m = jnp.max(s, axis=-1, keepdims=True)
                    p = jnp.exp2(s - m)
                    new_m[u, rs] = jnp.broadcast_to(m, (16, HEAD_DIM))
                    new_l[u, rs] = jnp.broadcast_to(jnp.sum(p, axis=-1, keepdims=True), (16, HEAD_DIM))
                    prob[u, rs, 0:n] = p.astype(BF)
                pv = jnp.dot(prob[u, :, 0:n], vs[start : start + n, at[u]], preferred_element_type=F32)
                if first:
                    acc[:, at[u]] = pv
                    m_ref[heads[u]] = new_m[u]
                    l_ref[heads[u]] = new_l[u]
                else:
                    m1, m2 = m_ref[heads[u]], new_m[u]
                    m = jnp.maximum(m1, m2)
                    a1, a2 = jnp.exp2(m1 - m), jnp.exp2(m2 - m)
                    total = a1 * l_ref[heads[u]] + a2 * new_l[u]
                    joined = a1 * acc[:, at[u]] + a2 * pv
                    if last:
                        qs[:, at[u]] = (joined / total).astype(BF)
                    else:
                        acc[:, at[u]] = joined
                        m_ref[heads[u]] = m
                        l_ref[heads[u]] = total

    def each(fn, slots=(0, 1)):
        for slot in slots:
            pl.when(frames[slot][0])(functools.partial(fn, slot))

    loads[0].wait()
    qs[...] = rms(jnp.dot(xs[0:TOKENS, :], wq[...], preferred_element_type=F32), row(qgain_ref))
    loads[1].wait()
    keys_of(0, 256)
    y_sent(0)
    y_start(1)
    loads[2].wait()
    bias[...] = jnp.minimum(bias_in[...].astype(F32), extra).astype(BF)
    loads[3].wait()
    values_of(0, 256)

    def columns_on(slot):
        y_arrived(0, slot).wait_recv()
        h_start(slot + 1, (1,))

    each(columns_on)
    attend(0, 256, True, False)
    keys_of(352, 96)
    values_of(352, 96)
    h_wait(0, (0, 1))
    y_start(2)
    pack(0)
    h_start(0, (2, 3))
    keys_of(256, 96)
    values_of(256, 96)
    each(lambda slot: y_arrived(1, slot).wait_recv())
    y_start(3)
    keys_of(448, 224)
    values_of(448, 224)

    def rows_on(slot):
        y_arrived(2, slot).wait_recv()
        h_wait(slot + 1, (0,))
        pack(slot + 1)
        h_start(slot + 1, (2, 3))

    each(rows_on)
    h_wait(0, (2, 3))
    keys_of(672, 352)
    values_of(672, 352)
    attend(256, 768, False, False)
    each(lambda slot: y_arrived(3, slot).wait_recv())
    each(lambda slot: h_wait(slot + 1, (2, 3)))
    keys_of(1024, 512)
    values_of(1024, 512)
    attend(1024, 512, False, True)

    for chunk in (1, 2, 3):
        y_sent(chunk)
    h_sent(0, range(4))
    each(lambda slot: h_sent(slot + 1, (1, 2, 3)))
    loads[4].wait()
    stores = []
    for i in range(3):
        cols = slice(512 * i, 512 * i + 512)
        product = jnp.dot(qs[...], wo[:, cols], preferred_element_type=F32)
        staged[:, cols] = (product * gate_ref[cols].reshape(1, 512)).astype(BF)
        stores.append(pltpu.make_async_copy(staged.at[:, cols], out_any.at[:, cols], o_sem.at[i]))
        stores[-1].start()
    for store in stores:
        store.wait()


def shards(latents, ada_shift, ada_scale, ada_gate, w_query, w_key, w_value, w_out, query_gain, key_gain):
    select, pack, bias = tables()
    vmem = pl.BlockSpec(memory_space=pltpu.VMEM)
    hbm = pl.BlockSpec(memory_space=pl.ANY)
    out = pl.pallas_call(
        kernel,
        out_shape=jax.ShapeDtypeStruct((TOKENS, D), BF),
        in_specs=[vmem] * 6 + [hbm] * 4 + [vmem] * 2 + [hbm],
        out_specs=hbm,
        scratch_shapes=[pltpu.VMEM((D, D), BF)] * 4
        + [
            pltpu.VMEM((KEYS, D), BF),
            pltpu.VMEM((KEYS, D), BF),
            pltpu.VMEM((KEYS, D), BF),
            pltpu.VMEM((TOKENS, D), BF),
            pltpu.VMEM((TOKENS, D), BF),
            pltpu.VMEM((3, 160, D), BF),
            pltpu.VMEM((TOKENS, KEYS), BF),
            pltpu.VMEM((TOKENS, KEYS), BF),
            pltpu.VMEM((TOKENS, D), F32),
            pltpu.VMEM((HEADS, TOKENS, HEAD_DIM), F32),
            pltpu.VMEM((HEADS, TOKENS, HEAD_DIM), F32),
            pltpu.VMEM((GROUP, TOKENS, 768), F32),
            pltpu.VMEM((GROUP, TOKENS, 768), BF),
            pltpu.VMEM((GROUP, TOKENS, HEAD_DIM), F32),
            pltpu.VMEM((GROUP, TOKENS, HEAD_DIM), F32),
            pltpu.SemaphoreType.DMA((5,)),
            pltpu.SemaphoreType.DMA((3,)),
            pltpu.SemaphoreType.DMA((4, 2)),
            pltpu.SemaphoreType.DMA((4, 2)),
            pltpu.SemaphoreType.DMA((3, 4)),
            pltpu.SemaphoreType.DMA((3, 4)),
        ],
        compiler_params=pltpu.CompilerParams(
            collective_id=0, has_side_effects=True, vmem_limit_bytes=62 * 2**20
        ),
        cost_estimate=pl.CostEstimate(flops=2 * 10**10, bytes_accessed=2 * 10**7, transcendentals=5 * 10**6),
    )(
        latents.reshape(TOKENS, D), ada_shift, ada_scale, ada_gate, query_gain, key_gain,
        w_query, w_key, w_value, w_out,
        jnp.asarray(select, BF), jnp.asarray(pack, BF), jnp.asarray(bias, BF),
    )
    return out.reshape(latents.shape)


def solution(mesh):
    return jax.shard_map(
        shards,
        mesh=mesh,
        in_specs=(P("tm", "lat", "lon", None),) + (P(),) * 9,
        out_specs=P("tm", "lat", "lon", None),
        check_vma=False,
    )
```

```python
import functools
import math

import jax
import jax.numpy as jnp
import numpy as np
from jax import lax
from jax.experimental import pallas as pl
from jax.experimental.pallas import tpu as pltpu
from jax.sharding import PartitionSpec as P

HEADS = 12
HEAD_DIM = 128
D = 1536
SIDE = 16
TOKENS = SIDE * SIDE
KEYS = 1536
BF = jnp.bfloat16
F32 = jnp.float32
MESH = pl.DeviceIdType.MESH
MASKED = -1e30
GROUP = 6
SCALE = HEAD_DIM ** (-0.5) * math.log2(math.e)

CHUNKS = ((0, 48), (48, 112), None, (160, 96))
CHUNK_ROWS = (48, 112, 48, 96)
CHUNK_AT = ((352, 400), (448, 560), (672, 720), (1024, 1120))
HALO_E = 304
WEST_AT = (256, 768, 816)
ROWS_AT = (864, 1216, 1376)


def center_order():
    order = [(r, c) for c in (13, 14, 15, 0, 1, 2) for r in range(16)]
    order += [(r, c) for r in (0, 1, 2) for c in range(3, 13)]
    order += [(r, c) for r in (13, 14, 15) for c in range(3, 13)]
    order += [(r, c) for r in range(3, 13) for c in range(3, 13)]
    return order


def tables():
    order = center_order()
    natural = [(r, c) for r in range(SIDE) for c in range(SIDE)]
    west = [(r, c - 16) for c in (13, 14, 15) for r in range(16)]
    east = [(r, c + 16) for c in (0, 1, 2) for r in range(16)]
    bands = [[(r, c) for r in rows for c in range(-3, 19)] + [None] * 14 for rows in ((0, 1, 2), (13, 14, 15))]
    north = [p and (p[0] - 16, p[1]) for p in bands[1]]
    south = [p and (p[0] + 16, p[1]) for p in bands[0]]
    select = np.zeros((TOKENS, TOKENS), np.float32)
    for i, (r, c) in enumerate(order):
        select[i, r * SIDE + c] = 1
    where = {p: i for i, p in enumerate(order[:160] + west + east)}
    pack = np.zeros((160, 256), np.float32)
    for i, p in enumerate(bands[0] + bands[1]):
        if p is not None:
            pack[i, where[p]] = 1
    keys = [None] * KEYS

    def place(start, cells):
        keys[start : start + len(cells)] = cells

    place(0, natural)
    place(HALO_E, east)
    for chunk, spots in zip(CHUNKS, CHUNK_AT):
        for spot in spots:
            place(spot, order[chunk[0] : sum(chunk)] if chunk else east)
    for slot in range(3):
        place(WEST_AT[slot], west)
        place(ROWS_AT[slot], north + south)
    bias = np.full((TOKENS, KEYS), MASKED, np.float32)
    for j, p in enumerate(keys):
        if p is None:
            continue
        for i, (r, c) in enumerate(natural):
            if abs(r - p[0]) <= 3 and abs(c - p[1]) <= 3:
                bias[i, j] = 0
    return select, pack, bias


def kernel(
    x_any, shift_any, scale_any, qgain_any, kgain_any, wq_any, wk_any, wv_any, select_any, pack_any, bias_any,
    wo_any, gate_any, out_any,
    x_ref, shift_ref, scale_ref, qgain_ref, kgain_ref, wq, wk, wv, select_ref, pack_ref, wo, gate_ref, xs, ks, vs, qs, staged, packed, bias_in, bias, acc, m_ref, l_ref, score, prob, new_m, new_l,
    w_sem, o_sem, y_send, y_recv, h_send, h_recv,
):
    t, a, o = lax.axis_index("tm"), lax.axis_index("lat"), lax.axis_index("lon")
    west, east = lax.rem(o + 7, 8), lax.rem(o + 1, 8)
    has_prev, has_next = t > 0, t < 3
    has_north, has_south = a > 0, a < 3
    dirs = (
        (None, (t, a, west)), (None, (t, a, east)),
        (has_north, (t, a - 1, o)), (has_south, (t, a + 1, o)),
    )
    opposite = (1, 0, 3, 2)
    frames = ((has_prev, (t - 1, a, o)), (has_next, (t + 1, a, o)))

    def when(cond, fn):
        if cond is None:
            fn()
        else:
            pl.when(cond)(fn)

    barrier = pltpu.get_barrier_semaphore()
    for cond, dev in dirs + frames:
        when(cond, lambda dev=dev: pl.semaphore_signal(barrier, inc=1, device_id=dev, device_id_type=MESH))

    pairs = (
        (x_any, x_ref), (shift_any, shift_ref), (scale_any, scale_ref), (select_any, select_ref),
        (wq_any, wq), (qgain_any, qgain_ref), (wk_any, wk), (kgain_any, kgain_ref),
        (bias_any, bias_in), (wv_any, wv), (pack_any, pack_ref), (wo_any, wo), (gate_any, gate_ref),
    )
    loads = [pltpu.make_async_copy(src, dst, w_sem.at[i]) for i, (src, dst) in enumerate(pairs)]
    for load in loads[:3]:
        load.start()

    one = lambda c: jnp.where(c, 1, 0)

    row = lambda ref: ref[...].reshape(1, D)
    for load in loads[:3]:
        load.wait()
    for load in loads[3:]:
        load.start()
    shift, scale = row(shift_ref), 1.0 + row(scale_ref)

    for i in range(8):
        rows = slice(32 * i, 32 * i + 32)
        v = x_ref[rows, :].astype(F32)
        centred = v - jnp.mean(v, axis=-1, keepdims=True)
        var = jnp.mean(centred * centred, axis=-1, keepdims=True)
        xs[rows, :] = (centred * lax.rsqrt(var + 1e-06) * scale + shift).astype(BF)

    loads[3].wait()
    staged[...] = jnp.dot(select_ref[...], xs[0:TOKENS, :], preferred_element_type=F32).astype(BF)
    pl.semaphore_wait(barrier, 2 + one(has_prev) + one(has_next) + one(has_north) + one(has_south))

    def y_copy(chunk, side):
        n, dst = CHUNK_ROWS[chunk], CHUNK_AT[chunk][1 - side]
        if CHUNKS[chunk]:
            src = staged.at[CHUNKS[chunk][0] : sum(CHUNKS[chunk])]
        else:
            src = xs.at[HALO_E : HALO_E + n]
        return pltpu.make_async_remote_copy(
            src_ref=src, dst_ref=xs.at[dst : dst + n],
            send_sem=y_send.at[chunk, side], recv_sem=y_recv.at[chunk, 1 - side],
            device_id=frames[side][1], device_id_type=MESH,
        )

    def y_start(chunk):
        for side in range(2):
            when(frames[side][0], lambda side=side: y_copy(chunk, side).start())

    def y_arrived(chunk, slot):
        n, dst = CHUNK_ROWS[chunk], CHUNK_AT[chunk][slot]
        return pltpu.make_async_remote_copy(
            src_ref=xs.at[dst : dst + n], dst_ref=xs.at[dst : dst + n],
            send_sem=y_send.at[chunk, slot], recv_sem=y_recv.at[chunk, slot],
            device_id=frames[slot][1], device_id_type=MESH,
        )

    def piece(slot, d):
        if d == 0:
            return WEST_AT[slot], 48
        if d == 1:
            return HALO_E, 48
        return ROWS_AT[slot] + 80 * (d - 2), 80

    def h_copy(slot, d):
        dst, n = piece(slot, opposite[d])
        if d >= 2:
            src = packed.at[slot, 80 * (d - 2) : 80 * (d - 1)]
        elif slot == 0:
            src = staged.at[48 - 48 * d : 96 - 48 * d]
        else:
            src = xs.at[CHUNK_AT[0][slot - 1] : CHUNK_AT[0][slot - 1] + 48]
        return pltpu.make_async_remote_copy(
            src_ref=src, dst_ref=xs.at[dst : dst + n],
            send_sem=h_send.at[slot, d], recv_sem=h_recv.at[slot, opposite[d]],
            device_id=dirs[d][1], device_id_type=MESH,
        )

    def h_arrived(slot, d):
        dst, n = piece(slot, d)
        return pltpu.make_async_remote_copy(
            src_ref=xs.at[dst : dst + n], dst_ref=xs.at[dst : dst + n],
            send_sem=h_send.at[slot, d], recv_sem=h_recv.at[slot, d],
            device_id=dirs[d][1], device_id_type=MESH,
        )

    def h_start(slot, which):
        for d in which:
            when(dirs[d][0], lambda d=d: h_copy(slot, d).start())

    def h_wait(slot, which):
        for d in which:
            when(dirs[d][0], lambda d=d: h_arrived(slot, d).wait_recv())

    def y_sent(chunk):
        for side in range(2):
            when(frames[side][0], lambda side=side: y_copy(chunk, side).wait_send())

    def h_sent(slot, which):
        for d in which:
            when(dirs[d][0], lambda d=d: h_copy(slot, d).wait_send())

    def pack(slot):
        if slot == 0:
            parts = [staged[0:160, :], xs[256:352, :]]
        else:
            spots = [(CHUNK_AT[k][slot - 1], CHUNK_ROWS[k]) for k in range(3)]
            spots.insert(2, (WEST_AT[slot], 48))
            parts = [xs[p : p + n, :] for p, n in spots]
        edge = jnp.concatenate(parts, axis=0)
        packed[slot] = jnp.dot(pack_ref[...], edge, preferred_element_type=F32).astype(BF)

    y_start(0)
    h_start(0, (0, 1))

    def clear(start, n):
        xs[start : start + n, :] = jnp.zeros((n, D), BF)

    for slot in range(2):
        def absent(slot=slot):
            for n, c in zip(CHUNK_ROWS, CHUNK_AT):
                clear(c[slot], n)
            clear(WEST_AT[slot + 1], 48)
            clear(ROWS_AT[slot + 1], 160)
        pl.when(jnp.logical_not(frames[slot][0]))(absent)
    for d in (2, 3):
        def edge_clear(d=d):
            for slot in range(3):
                present = None if slot == 0 else frames[slot - 1][0]
                start, n = piece(slot, d)
                when(present, lambda start=start, n=n: clear(start, n))
        pl.when(jnp.logical_not(dirs[d][0]))(edge_clear)

    j = lax.broadcasted_iota(jnp.int32, (1, KEYS), 1)
    extra = jnp.zeros((1, KEYS), F32)

    def bar(extra, cond, start, n):
        off = (j >= start) & (j < start + n) & jnp.logical_not(cond)
        return jnp.where(off, MASKED, extra)

    for slot in range(2):
        for n, c in zip(CHUNK_ROWS, CHUNK_AT):
            extra = bar(extra, frames[slot][0], c[slot], n)
        extra = bar(extra, frames[slot][0], WEST_AT[slot + 1], 48)
        extra = bar(extra, frames[slot][0], ROWS_AT[slot + 1], 160)
    for slot in range(3):
        for d in (2, 3):
            extra = bar(extra, dirs[d][0], *piece(slot, d))

    def rms(p, gain):
        ms = jnp.mean(p * p, axis=-1, keepdims=True)
        return (p * lax.rsqrt(ms + 1e-06) * gain).astype(BF)

    def keys_of(start, n):
        p = jnp.dot(xs[start : start + n, :], wk[...], preferred_element_type=F32)
        ks[start : start + n, :] = rms(p, row(kgain_ref))

    def values_of(start, n):
        vs[start : start + n, :] = jnp.dot(
            xs[start : start + n, :], wv[...], preferred_element_type=F32
        ).astype(BF)

    def attend(start, n, first, last):
        @pl.loop(0, HEADS // GROUP)
        def _(g):
            heads = [g * GROUP + u for u in range(GROUP)]
            at = [pl.ds(pl.multiple_of(h * HEAD_DIM, HEAD_DIM), HEAD_DIM) for h in heads]
            for u in range(GROUP):
                score[u, :, 0:n] = lax.dot_general(
                    qs[:, at[u]], ks[start : start + n, at[u]], (((1,), (1,)), ((), ())), preferred_element_type=F32
                )
            for u in range(GROUP):
                for r in range(0, TOKENS, 16):
                    rs = slice(r, r + 16)
                    s = score[u, rs, 0:n] * SCALE + bias[rs, start : start + n].astype(F32)
                    m = jnp.max(s, axis=-1, keepdims=True)
                    p = jnp.exp2(s - m)
                    new_m[u, rs] = jnp.broadcast_to(m, (16, HEAD_DIM))
                    new_l[u, rs] = jnp.broadcast_to(jnp.sum(p, axis=-1, keepdims=True), (16, HEAD_DIM))
                    prob[u, rs, 0:n] = p.astype(BF)
                pv = jnp.dot(prob[u, :, 0:n], vs[start : start + n, at[u]], preferred_element_type=F32)
                if first:
                    acc[:, at[u]] = pv
                    m_ref[heads[u]] = new_m[u]
                    l_ref[heads[u]] = new_l[u]
                else:
                    m1, m2 = m_ref[heads[u]], new_m[u]
                    m = jnp.maximum(m1, m2)
                    a1, a2 = jnp.exp2(m1 - m), jnp.exp2(m2 - m)
                    total = a1 * l_ref[heads[u]] + a2 * new_l[u]
                    joined = a1 * acc[:, at[u]] + a2 * pv
                    if last:
                        qs[:, at[u]] = (joined / total).astype(BF)
                    else:
                        acc[:, at[u]] = joined
                        m_ref[heads[u]] = m
                        l_ref[heads[u]] = total

    def each(fn, slots=(0, 1)):
        for slot in slots:
            pl.when(frames[slot][0])(functools.partial(fn, slot))

    loads[4].wait()
    loads[5].wait()
    qs[...] = rms(jnp.dot(xs[0:TOKENS, :], wq[...], preferred_element_type=F32), row(qgain_ref))
    loads[6].wait()
    loads[7].wait()
    keys_of(0, 256)
    y_sent(0)
    y_start(1)
    loads[8].wait()
    bias[...] = jnp.minimum(bias_in[...].astype(F32), extra).astype(BF)
    loads[9].wait()
    loads[10].wait()
    values_of(0, 256)

    def columns_on(slot):
        y_arrived(0, slot).wait_recv()
        h_start(slot + 1, (1,))

    each(columns_on)
    attend(0, 256, True, False)
    keys_of(352, 96)
    values_of(352, 96)
    h_wait(0, (0, 1))
    y_start(2)
    pack(0)
    h_start(0, (2, 3))
    keys_of(256, 96)
    values_of(256, 96)
    each(lambda slot: y_arrived(1, slot).wait_recv())
    keys_of(448, 224)
    values_of(448, 224)

    def rows_on(slot):
        y_arrived(2, slot).wait_recv()
        h_wait(slot + 1, (0,))
        pack(slot + 1)
        h_start(slot + 1, (2, 3))

    each(rows_on)
    y_start(3)
    h_wait(0, (2, 3))
    keys_of(672, 352)
    values_of(672, 352)
    attend(256, 768, False, False)
    each(lambda slot: y_arrived(3, slot).wait_recv())
    each(lambda slot: h_wait(slot + 1, (2, 3)))
    keys_of(1024, 512)
    values_of(1024, 512)
    attend(1024, 512, False, True)

    for chunk in (1, 2, 3):
        y_sent(chunk)
    h_sent(0, range(4))
    each(lambda slot: h_sent(slot + 1, (1, 2, 3)))
    for load in loads[11:]:
        load.wait()
    stores = []
    for i in range(3):
        cols = slice(512 * i, 512 * i + 512)
        product = jnp.dot(qs[...], wo[:, cols], preferred_element_type=F32)
        staged[:, cols] = (product * gate_ref[cols].reshape(1, 512)).astype(BF)
        stores.append(pltpu.make_async_copy(staged.at[:, cols], out_any.at[:, cols], o_sem.at[i]))
        stores[-1].start()
    for store in stores:
        store.wait()


def shards(latents, ada_shift, ada_scale, ada_gate, w_query, w_key, w_value, w_out, query_gain, key_gain):
    select, pack, bias = tables()
    hbm = pl.BlockSpec(memory_space=pl.ANY)
    vector = pltpu.VMEM((D,), F32)
    square = pltpu.VMEM((D, D), BF)
    out = pl.pallas_call(
        kernel,
        out_shape=jax.ShapeDtypeStruct((TOKENS, D), BF),
        in_specs=[hbm] * 13,
        out_specs=hbm,
        scratch_shapes=[pltpu.VMEM((TOKENS, D), BF)]
        + [vector] * 4
        + [square] * 3
        + [
            pltpu.VMEM((TOKENS, TOKENS), BF),
            pltpu.VMEM((160, TOKENS), BF),
            square,
            vector,
            pltpu.VMEM((KEYS, D), BF),
            pltpu.VMEM((KEYS, D), BF),
            pltpu.VMEM((KEYS, D), BF),
            pltpu.VMEM((TOKENS, D), BF),
            pltpu.VMEM((TOKENS, D), BF),
            pltpu.VMEM((3, 160, D), BF),
            pltpu.VMEM((TOKENS, KEYS), BF),
            pltpu.VMEM((TOKENS, KEYS), BF),
            pltpu.VMEM((TOKENS, D), F32),
            pltpu.VMEM((HEADS, TOKENS, HEAD_DIM), F32),
            pltpu.VMEM((HEADS, TOKENS, HEAD_DIM), F32),
            pltpu.VMEM((GROUP, TOKENS, 768), F32),
            pltpu.VMEM((GROUP, TOKENS, 768), BF),
            pltpu.VMEM((GROUP, TOKENS, HEAD_DIM), F32),
            pltpu.VMEM((GROUP, TOKENS, HEAD_DIM), F32),
            pltpu.SemaphoreType.DMA((13,)),
            pltpu.SemaphoreType.DMA((3,)),
            pltpu.SemaphoreType.DMA((4, 2)),
            pltpu.SemaphoreType.DMA((4, 2)),
            pltpu.SemaphoreType.DMA((3, 4)),
            pltpu.SemaphoreType.DMA((3, 4)),
        ],
        compiler_params=pltpu.CompilerParams(
            collective_id=0, has_side_effects=True, vmem_limit_bytes=62 * 2**20
        ),
        cost_estimate=pl.CostEstimate(flops=2 * 10**10, bytes_accessed=2 * 10**7, transcendentals=5 * 10**6),
    )(
        latents.reshape(TOKENS, D), ada_shift, ada_scale, query_gain, key_gain, w_query, w_key, w_value,
        jnp.asarray(select, BF), jnp.asarray(pack, BF), jnp.asarray(bias, BF),
        w_out, ada_gate,
    )
    return out.reshape(latents.shape)


def solution(mesh):
    return jax.shard_map(
        shards,
        mesh=mesh,
        in_specs=(P("tm", "lat", "lon", None),) + (P(),) * 9,
        out_specs=P("tm", "lat", "lon", None),
        check_vma=False,
    )
```

```python
import functools
import math

import jax
import jax.numpy as jnp
import numpy as np
from jax import lax
from jax.experimental import pallas as pl
from jax.experimental.pallas import tpu as pltpu
from jax.sharding import PartitionSpec as P

HEADS = 12
HEAD_DIM = 128
D = 1536
SIDE = 16
TOKENS = SIDE * SIDE
KEYS = 1536
BF = jnp.bfloat16
F32 = jnp.float32
MESH = pl.DeviceIdType.MESH
MASKED = -1e30
GROUP = 6
SCALE = HEAD_DIM ** (-0.5) * math.log2(math.e)

CHUNKS = ((0, 48), (48, 112), None, (160, 96))
CHUNK_ROWS = (48, 112, 48, 96)
CHUNK_AT = ((352, 400), (448, 560), (672, 720), (1024, 1120))
HALO_E = 304
WEST_AT = (256, 768, 816)
ROWS_AT = (864, 1216, 1376)


def center_order():
    order = [(r, c) for c in (13, 14, 15, 0, 1, 2) for r in range(16)]
    order += [(r, c) for r in (0, 1, 2) for c in range(3, 13)]
    order += [(r, c) for r in (13, 14, 15) for c in range(3, 13)]
    order += [(r, c) for r in range(3, 13) for c in range(3, 13)]
    return order


def tables():
    order = center_order()
    natural = [(r, c) for r in range(SIDE) for c in range(SIDE)]
    west = [(r, c - 16) for c in (13, 14, 15) for r in range(16)]
    east = [(r, c + 16) for c in (0, 1, 2) for r in range(16)]
    bands = [[(r, c) for r in rows for c in range(-3, 19)] + [None] * 14 for rows in ((0, 1, 2), (13, 14, 15))]
    north = [p and (p[0] - 16, p[1]) for p in bands[1]]
    south = [p and (p[0] + 16, p[1]) for p in bands[0]]
    select = np.zeros((TOKENS, TOKENS), np.float32)
    for i, (r, c) in enumerate(order):
        select[i, r * SIDE + c] = 1
    where = {p: i for i, p in enumerate(order[:160] + west + east)}
    pack = np.zeros((160, 256), np.float32)
    for i, p in enumerate(bands[0] + bands[1]):
        if p is not None:
            pack[i, where[p]] = 1
    keys = [None] * KEYS

    def place(start, cells):
        keys[start : start + len(cells)] = cells

    place(0, natural)
    place(HALO_E, east)
    for chunk, spots in zip(CHUNKS, CHUNK_AT):
        for spot in spots:
            place(spot, order[chunk[0] : sum(chunk)] if chunk else east)
    for slot in range(3):
        place(WEST_AT[slot], west)
        place(ROWS_AT[slot], north + south)
    bias = np.full((TOKENS, KEYS), MASKED, np.float32)
    for j, p in enumerate(keys):
        if p is None:
            continue
        for i, (r, c) in enumerate(natural):
            if abs(r - p[0]) <= 3 and abs(c - p[1]) <= 3:
                bias[i, j] = 0
    return select, pack, bias


def kernel(
    x_any, shift_any, scale_any, qgain_any, kgain_any, wq_any, wk_any, wv_any, select_any, pack_any, bias_any,
    wo_any, gate_any, out_any,
    x_ref, shift_ref, scale_ref, qgain_ref, kgain_ref, wq, wk, wv, select_ref, pack_ref, wo, gate_ref, xs, ks, vs, qs, staged, packed, bias_in, bias, acc, m_ref, l_ref, score, prob, new_m, new_l,
    w_sem, o_sem, y_send, y_recv, h_send, h_recv,
):
    t, a, o = lax.axis_index("tm"), lax.axis_index("lat"), lax.axis_index("lon")
    west, east = lax.rem(o + 7, 8), lax.rem(o + 1, 8)
    has_prev, has_next = t > 0, t < 3
    has_north, has_south = a > 0, a < 3
    dirs = (
        (None, (t, a, west)), (None, (t, a, east)),
        (has_north, (t, a - 1, o)), (has_south, (t, a + 1, o)),
    )
    opposite = (1, 0, 3, 2)
    frames = ((has_prev, (t - 1, a, o)), (has_next, (t + 1, a, o)))

    def when(cond, fn):
        if cond is None:
            fn()
        else:
            pl.when(cond)(fn)

    barrier = pltpu.get_barrier_semaphore()
    for cond, dev in dirs + frames:
        when(cond, lambda dev=dev: pl.semaphore_signal(barrier, inc=1, device_id=dev, device_id_type=MESH))

    pairs = (
        (x_any, x_ref), (shift_any, shift_ref), (scale_any, scale_ref), (select_any, select_ref),
        (wq_any, wq), (qgain_any, qgain_ref), (wk_any, wk), (kgain_any, kgain_ref),
        (bias_any, bias_in), (wv_any, wv), (pack_any, pack_ref), (wo_any, wo), (gate_any, gate_ref),
    )
    loads = [pltpu.make_async_copy(src, dst, w_sem.at[i]) for i, (src, dst) in enumerate(pairs)]
    for load in loads[:3]:
        load.start()

    one = lambda c: jnp.where(c, 1, 0)

    row = lambda ref: ref[...].reshape(1, D)
    for load in loads[:3]:
        load.wait()
    for load in loads[3:]:
        load.start()
    shift, scale = row(shift_ref), 1.0 + row(scale_ref)

    for i in range(8):
        rows = slice(32 * i, 32 * i + 32)
        v = x_ref[rows, :].astype(F32)
        centred = v - jnp.mean(v, axis=-1, keepdims=True)
        var = jnp.mean(centred * centred, axis=-1, keepdims=True)
        xs[rows, :] = (centred * lax.rsqrt(var + 1e-06) * scale + shift).astype(BF)

    loads[3].wait()
    staged[...] = jnp.dot(select_ref[...], xs[0:TOKENS, :], preferred_element_type=F32).astype(BF)
    pl.semaphore_wait(barrier, 2 + one(has_prev) + one(has_next) + one(has_north) + one(has_south))

    def y_copy(chunk, side):
        n, dst = CHUNK_ROWS[chunk], CHUNK_AT[chunk][1 - side]
        if CHUNKS[chunk]:
            src = staged.at[CHUNKS[chunk][0] : sum(CHUNKS[chunk])]
        else:
            src = xs.at[HALO_E : HALO_E + n]
        return pltpu.make_async_remote_copy(
            src_ref=src, dst_ref=xs.at[dst : dst + n],
            send_sem=y_send.at[chunk, side], recv_sem=y_recv.at[chunk, 1 - side],
            device_id=frames[side][1], device_id_type=MESH,
        )

    def y_start(chunk):
        for side in range(2):
            when(frames[side][0], lambda side=side: y_copy(chunk, side).start())

    def y_arrived(chunk, slot):
        n, dst = CHUNK_ROWS[chunk], CHUNK_AT[chunk][slot]
        return pltpu.make_async_remote_copy(
            src_ref=xs.at[dst : dst + n], dst_ref=xs.at[dst : dst + n],
            send_sem=y_send.at[chunk, slot], recv_sem=y_recv.at[chunk, slot],
            device_id=frames[slot][1], device_id_type=MESH,
        )

    def piece(slot, d):
        if d == 0:
            return WEST_AT[slot], 48
        if d == 1:
            return HALO_E, 48
        return ROWS_AT[slot] + 80 * (d - 2), 80

    def h_copy(slot, d):
        dst, n = piece(slot, opposite[d])
        if d >= 2:
            src = packed.at[slot, 80 * (d - 2) : 80 * (d - 1)]
        elif slot == 0:
            src = staged.at[48 - 48 * d : 96 - 48 * d]
        else:
            src = xs.at[CHUNK_AT[0][slot - 1] : CHUNK_AT[0][slot - 1] + 48]
        return pltpu.make_async_remote_copy(
            src_ref=src, dst_ref=xs.at[dst : dst + n],
            send_sem=h_send.at[slot, d], recv_sem=h_recv.at[slot, opposite[d]],
            device_id=dirs[d][1], device_id_type=MESH,
        )

    def h_arrived(slot, d):
        dst, n = piece(slot, d)
        return pltpu.make_async_remote_copy(
            src_ref=xs.at[dst : dst + n], dst_ref=xs.at[dst : dst + n],
            send_sem=h_send.at[slot, d], recv_sem=h_recv.at[slot, d],
            device_id=dirs[d][1], device_id_type=MESH,
        )

    def h_start(slot, which):
        for d in which:
            when(dirs[d][0], lambda d=d: h_copy(slot, d).start())

    def h_wait(slot, which):
        for d in which:
            when(dirs[d][0], lambda d=d: h_arrived(slot, d).wait_recv())

    def y_sent(chunk):
        for side in range(2):
            when(frames[side][0], lambda side=side: y_copy(chunk, side).wait_send())

    def h_sent(slot, which):
        for d in which:
            when(dirs[d][0], lambda d=d: h_copy(slot, d).wait_send())

    def pack(slot):
        if slot == 0:
            parts = [staged[0:160, :], xs[256:352, :]]
        else:
            spots = [(CHUNK_AT[k][slot - 1], CHUNK_ROWS[k]) for k in range(3)]
            spots.insert(2, (WEST_AT[slot], 48))
            parts = [xs[p : p + n, :] for p, n in spots]
        edge = jnp.concatenate(parts, axis=0)
        packed[slot] = jnp.dot(pack_ref[...], edge, preferred_element_type=F32).astype(BF)

    y_start(0)
    h_start(0, (0, 1))

    def clear(start, n):
        xs[start : start + n, :] = jnp.zeros((n, D), BF)

    for slot in range(2):
        def absent(slot=slot):
            for n, c in zip(CHUNK_ROWS, CHUNK_AT):
                clear(c[slot], n)
            clear(WEST_AT[slot + 1], 48)
            clear(ROWS_AT[slot + 1], 160)
        pl.when(jnp.logical_not(frames[slot][0]))(absent)
    for d in (2, 3):
        def edge_clear(d=d):
            for slot in range(3):
                present = None if slot == 0 else frames[slot - 1][0]
                start, n = piece(slot, d)
                when(present, lambda start=start, n=n: clear(start, n))
        pl.when(jnp.logical_not(dirs[d][0]))(edge_clear)

    j = lax.broadcasted_iota(jnp.int32, (1, KEYS), 1)
    extra = jnp.zeros((1, KEYS), F32)

    def bar(extra, cond, start, n):
        off = (j >= start) & (j < start + n) & jnp.logical_not(cond)
        return jnp.where(off, MASKED, extra)

    for slot in range(2):
        for n, c in zip(CHUNK_ROWS, CHUNK_AT):
            extra = bar(extra, frames[slot][0], c[slot], n)
        extra = bar(extra, frames[slot][0], WEST_AT[slot + 1], 48)
        extra = bar(extra, frames[slot][0], ROWS_AT[slot + 1], 160)
    for slot in range(3):
        for d in (2, 3):
            extra = bar(extra, dirs[d][0], *piece(slot, d))

    def rms(p, gain):
        ms = jnp.mean(p * p, axis=-1, keepdims=True)
        return (p * lax.rsqrt(ms + 1e-06) * gain).astype(BF)

    def keys_of(start, n):
        p = jnp.dot(xs[start : start + n, :], wk[...], preferred_element_type=F32)
        ks[start : start + n, :] = rms(p, row(kgain_ref))

    def values_of(start, n):
        vs[start : start + n, :] = jnp.dot(
            xs[start : start + n, :], wv[...], preferred_element_type=F32
        ).astype(BF)

    def attend(start, n, first, last):
        for g in range(HEADS // GROUP):
            heads = [g * GROUP + u for u in range(GROUP)]
            at = [pl.ds(h * HEAD_DIM, HEAD_DIM) for h in heads]
            for u in range(GROUP):
                score[u, :, 0:n] = lax.dot_general(
                    qs[:, at[u]], ks[start : start + n, at[u]], (((1,), (1,)), ((), ())), preferred_element_type=F32
                )
            for u in range(GROUP):
                for r in range(0, TOKENS, 16):
                    rs = slice(r, r + 16)
                    s = score[u, rs, 0:n] * SCALE + bias[rs, start : start + n].astype(F32)
                    m = jnp.max(s, axis=-1, keepdims=True)
                    p = jnp.exp2(s - m)
                    new_m[u, rs] = jnp.broadcast_to(m, (16, HEAD_DIM))
                    new_l[u, rs] = jnp.broadcast_to(jnp.sum(p, axis=-1, keepdims=True), (16, HEAD_DIM))
                    prob[u, rs, 0:n] = p.astype(BF)
                pv = jnp.dot(prob[u, :, 0:n], vs[start : start + n, at[u]], preferred_element_type=F32)
                if first:
                    acc[:, at[u]] = pv
                    m_ref[heads[u]] = new_m[u]
                    l_ref[heads[u]] = new_l[u]
                else:
                    m1, m2 = m_ref[heads[u]], new_m[u]
                    m = jnp.maximum(m1, m2)
                    a1, a2 = jnp.exp2(m1 - m), jnp.exp2(m2 - m)
                    total = a1 * l_ref[heads[u]] + a2 * new_l[u]
                    joined = a1 * acc[:, at[u]] + a2 * pv
                    if last:
                        qs[:, at[u]] = (joined / total).astype(BF)
                    else:
                        acc[:, at[u]] = joined
                        m_ref[heads[u]] = m
                        l_ref[heads[u]] = total

    def each(fn, slots=(0, 1)):
        for slot in slots:
            pl.when(frames[slot][0])(functools.partial(fn, slot))

    loads[4].wait()
    loads[5].wait()
    qs[...] = rms(jnp.dot(xs[0:TOKENS, :], wq[...], preferred_element_type=F32), row(qgain_ref))
    loads[6].wait()
    loads[7].wait()
    keys_of(0, 256)
    y_sent(0)
    y_start(1)
    loads[8].wait()
    bias[...] = jnp.minimum(bias_in[...].astype(F32), extra).astype(BF)
    loads[9].wait()
    loads[10].wait()
    values_of(0, 256)

    def columns_on(slot):
        y_arrived(0, slot).wait_recv()
        h_start(slot + 1, (1,))

    each(columns_on)
    attend(0, 256, True, False)
    keys_of(352, 96)
    values_of(352, 96)
    h_wait(0, (0, 1))
    y_start(2)
    pack(0)
    h_start(0, (2, 3))
    keys_of(256, 96)
    values_of(256, 96)
    each(lambda slot: y_arrived(1, slot).wait_recv())
    keys_of(448, 224)
    values_of(448, 224)

    def rows_on(slot):
        y_arrived(2, slot).wait_recv()
        h_wait(slot + 1, (0,))
        pack(slot + 1)
        h_start(slot + 1, (2, 3))

    each(rows_on)
    y_start(3)
    h_wait(0, (2, 3))
    keys_of(672, 352)
    values_of(672, 352)
    attend(256, 768, False, False)
    each(lambda slot: y_arrived(3, slot).wait_recv())
    each(lambda slot: h_wait(slot + 1, (2, 3)))
    keys_of(1024, 512)
    values_of(1024, 512)
    attend(1024, 512, False, True)

    for chunk in (1, 2, 3):
        y_sent(chunk)
    h_sent(0, range(4))
    each(lambda slot: h_sent(slot + 1, (1, 2, 3)))
    for load in loads[11:]:
        load.wait()
    stores = []
    for i in range(3):
        cols = slice(512 * i, 512 * i + 512)
        product = jnp.dot(qs[...], wo[:, cols], preferred_element_type=F32)
        staged[:, cols] = (product * gate_ref[cols].reshape(1, 512)).astype(BF)
        stores.append(pltpu.make_async_copy(staged.at[:, cols], out_any.at[:, cols], o_sem.at[i]))
        stores[-1].start()
    for store in stores:
        store.wait()


def shards(latents, ada_shift, ada_scale, ada_gate, w_query, w_key, w_value, w_out, query_gain, key_gain):
    select, pack, bias = tables()
    hbm = pl.BlockSpec(memory_space=pl.ANY)
    vector = pltpu.VMEM((D,), F32)
    square = pltpu.VMEM((D, D), BF)
    out = pl.pallas_call(
        kernel,
        out_shape=jax.ShapeDtypeStruct((TOKENS, D), BF),
        in_specs=[hbm] * 13,
        out_specs=hbm,
        scratch_shapes=[pltpu.VMEM((TOKENS, D), BF)]
        + [vector] * 4
        + [square] * 3
        + [
            pltpu.VMEM((TOKENS, TOKENS), BF),
            pltpu.VMEM((160, TOKENS), BF),
            square,
            vector,
            pltpu.VMEM((KEYS, D), BF),
            pltpu.VMEM((KEYS, D), BF),
            pltpu.VMEM((KEYS, D), BF),
            pltpu.VMEM((TOKENS, D), BF),
            pltpu.VMEM((TOKENS, D), BF),
            pltpu.VMEM((3, 160, D), BF),
            pltpu.VMEM((TOKENS, KEYS), BF),
            pltpu.VMEM((TOKENS, KEYS), BF),
            pltpu.VMEM((TOKENS, D), F32),
            pltpu.VMEM((HEADS, TOKENS, HEAD_DIM), F32),
            pltpu.VMEM((HEADS, TOKENS, HEAD_DIM), F32),
            pltpu.VMEM((GROUP, TOKENS, 768), F32),
            pltpu.VMEM((GROUP, TOKENS, 768), BF),
            pltpu.VMEM((GROUP, TOKENS, HEAD_DIM), F32),
            pltpu.VMEM((GROUP, TOKENS, HEAD_DIM), F32),
            pltpu.SemaphoreType.DMA((13,)),
            pltpu.SemaphoreType.DMA((3,)),
            pltpu.SemaphoreType.DMA((4, 2)),
            pltpu.SemaphoreType.DMA((4, 2)),
            pltpu.SemaphoreType.DMA((3, 4)),
            pltpu.SemaphoreType.DMA((3, 4)),
        ],
        compiler_params=pltpu.CompilerParams(
            collective_id=0, has_side_effects=True, vmem_limit_bytes=62 * 2**20
        ),
        cost_estimate=pl.CostEstimate(flops=2 * 10**10, bytes_accessed=2 * 10**7, transcendentals=5 * 10**6),
    )(
        latents.reshape(TOKENS, D), ada_shift, ada_scale, query_gain, key_gain, w_query, w_key, w_value,
        jnp.asarray(select, BF), jnp.asarray(pack, BF), jnp.asarray(bias, BF),
        w_out, ada_gate,
    )
    return out.reshape(latents.shape)


def solution(mesh):
    return jax.shard_map(
        shards,
        mesh=mesh,
        in_specs=(P("tm", "lat", "lon", None),) + (P(),) * 9,
        out_specs=P("tm", "lat", "lon", None),
        check_vma=False,
    )
```
